512 devices in a mesh: frame: 8 (over z_lo, core), seq: 64 (over y, z_hi, x).
Axes of the slice: x: 4, y: 4, z: 16 (z_hi: 4, z_lo: 4; z = z_hi * 4 + z_lo), core: 2. Of those that a mesh axis runs over, the one named last changes fastest.
Arguments:
- queries: bfloat16 [64, 1024, 3072], P('frame', 'seq'), may hold values from -140 to 140
- keys: bfloat16 [64, 1024, 3072], P('frame', 'seq'), may hold values from -6 to 6
- values: bfloat16 [64, 1024, 3072], P('frame', 'seq'), may hold values from -6 to 6
- ref_keys: bfloat16 [1536, 3072], P(('frame', 'seq')), may hold values from -6 to 6
- ref_values: bfloat16 [1536, 3072], P(('frame', 'seq')), may hold values from -6 to 6
Outputs:
- attended: bfloat16 [64, 1024, 3072], P('frame', 'seq')
The draws below stay inside these ranges and needn't reach their ends.
All inputs are finite; a program needn't handle non-finite values.
Results may differ from the reference program's by a relative error of at most 0.0055.
Values may be sent and summed in bfloat16 or wider, within the bound.
No kernel may reach another device: no remote copies, remote signals or barrier semaphores. Data moves between devices by JAX's collectives and lax.ppermute only.
A program may use at most 64 MiB of HBM per device.

```python
import math
import jax
import jax.numpy as jnp
from jax import lax

H = 24
HD = 128
FRAMES = 64
FRAME_TOK = 1024
REF_TOK = 1536


def pair_base(key):
    full_shape = (FRAMES, FRAME_TOK, H * HD)
    base_normal = jax.random.truncated_normal(key, -6.0, 6.0, full_shape, jnp.float32)
    return base_normal


def draw_queries(key, part):
    base_normal = pair_base(key)
    key = jax.random.fold_in(key, 1)
    fresh_noise = jax.random.truncated_normal(key, -6.0, 6.0, base_normal.shape, jnp.float32)
    result = fresh_noise
    return result.astype(jnp.bfloat16)


def draw_keys(key, part):
    base_normal = pair_base(key)
    result = base_normal
    return result.astype(jnp.bfloat16)


def block_levels(own_key, dims, shards, smallest, high):
    level = 1.0
    for axis_at, shards_of in shards:
        heights = jax.random.uniform(jax.random.fold_in(jax.random.fold_in(own_key, 6), axis_at), (shards_of,), jnp.float32, smallest / len(shards), high / len(shards))
        level = level * jnp.repeat(jnp.exp(heights), dims[axis_at] // shards_of).reshape((-1,) + (1,) * (len(dims) - 1 - axis_at))
    return level


def bell_draw(rng, dims, deviation, bound, pieces=(), kind=jnp.bfloat16):
    drawn = deviation * jax.random.normal(rng, dims, jnp.float32)
    if pieces:
        drawn = drawn * block_levels(rng, dims, pieces, -0.22, 0.18)
    return jnp.clip(drawn, -bound, bound).astype(kind)


def setup_inputs(seed: int = 0) -> dict:
    key_list = jax.random.split(jax.random.key(seed), 6)
    return {
        "queries": draw_queries(jax.random.fold_in(key_list[5], 71), 0),
        "keys": draw_keys(jax.random.fold_in(key_list[5], 71), 0),
        "values": bell_draw(key_list[2], (FRAMES, FRAME_TOK, H * HD), 1.0, 6.0, ((0, 8), (1, 64))),
        "ref_keys": bell_draw(key_list[3], (REF_TOK, H * HD), 1.0, 6.0, ((0, 512),)),
        "ref_values": bell_draw(key_list[4], (REF_TOK, H * HD), 1.0, 6.0, ((0, 512),)),
    }


def normalized(scores, value_heads):
    highest = lax.optimization_barrier(jnp.max(scores, axis=-1, keepdims=True))
    weights = jnp.exp(scores - highest)
    totals = lax.optimization_barrier(jnp.sum(weights, axis=-1, keepdims=True))
    rounded = lax.optimization_barrier(weights.astype(jnp.bfloat16)).astype(jnp.float32)
    numerator = jnp.einsum('hqk,khd->qhd', rounded, value_heads)
    return numerator / jnp.transpose(totals, (1, 0, 2))

def reference(queries, keys, values, ref_keys, ref_values):
    scaling = 1.0 / math.sqrt(HD)
    ref_key_heads = ref_keys.astype(jnp.float32).reshape(REF_TOK, H, HD)
    ref_value_heads = ref_values.astype(jnp.float32).reshape(REF_TOK, H, HD)

    def spatial_frame(operands):
        query_frame, key_frame, value_frame = operands
        query_heads = query_frame.astype(jnp.float32).reshape(FRAME_TOK, H, HD)
        key_all = jnp.concatenate([key_frame.astype(jnp.float32).reshape(FRAME_TOK, H, HD), ref_key_heads], axis=0)
        value_all = jnp.concatenate([value_frame.astype(jnp.float32).reshape(FRAME_TOK, H, HD), ref_value_heads], axis=0)
        scores = jnp.einsum('qhd,khd->hqk', query_heads, key_all) * scaling
        return normalized(scores, value_all).reshape(FRAME_TOK, H * HD).astype(jnp.bfloat16)
    spatial = lax.map(spatial_frame, (queries, keys, values))

    def temporal_token(operands):
        query_token, key_token, value_token = operands
        query_heads = query_token.astype(jnp.float32).reshape(FRAMES, H, HD)
        key_heads = key_token.astype(jnp.float32).reshape(FRAMES, H, HD)
        value_heads = value_token.astype(jnp.float32).reshape(FRAMES, H, HD)
        scores = jnp.einsum('fhd,ghd->hfg', query_heads, key_heads) * scaling
        return normalized(scores, value_heads).reshape(FRAMES, H * HD).astype(jnp.bfloat16)
    temporal = lax.map(temporal_token, (jnp.swapaxes(queries, 0, 1), jnp.swapaxes(keys, 0, 1), jnp.swapaxes(values, 0, 1)))
    temporal = jnp.swapaxes(temporal, 0, 1)
    return (spatial.astype(jnp.float32) + temporal.astype(jnp.float32)).astype(jnp.bfloat16)
```

```python
import math

import jax
import jax.numpy as jnp
from jax import lax
from jax.experimental import pallas as pl
from jax.experimental.pallas import tpu as pltpu
from jax.sharding import Mesh, PartitionSpec as P

HD = 128
LOG2E = 1.4426950408889634
Z = ("zl1", "zl0", "zh")
YX = ("y", "x")
VMEM = pl.BlockSpec(memory_space=pltpu.VMEM)


def head_of(z_index, slot):
    zl1, zl0, zh = z_index // 8, (z_index // 4) % 2, z_index % 4
    pair = zh * 2 + zl1
    return pair * 3 + (1 if slot == 2 else 2 * zl0)


def frame_of(z_index, j, slot):
    zl0 = (z_index // 4) % 2
    return 4 * zl0 + j if slot == 2 else 2 * j + slot


def pack_kernel(q_ref, k_ref, v_ref, out_ref):
    for z in range(16):
        for j in range(4):
            for slot in range(3):
                frame = frame_of(z, j, slot)
                head = head_of(z, slot)
                for t, ref in enumerate((q_ref, k_ref, v_ref)):
                    out_ref[z, j, t, slot] = ref[frame, :, head * HD : (head + 1) * HD]


def pack_refs_kernel(key_ref, value_ref, out_ref):
    for z in range(16):
        for ab, slot in enumerate((0, 2)):
            head = head_of(z, slot)
            for t, ref in enumerate((key_ref, value_ref)):
                out_ref[z, t, ab] = ref[:, head * HD : (head + 1) * HD]


def unpack_kernel(in_ref, out_ref):
    for z in range(16):
        for j in range(4):
            for slot in range(3):
                frame = frame_of(z, j, slot)
                head = head_of(z, slot)
                out_ref[frame, :, head * HD : (head + 1) * HD] = in_ref[z, j, slot]


def spatial_kernel(x_ref, ref_ref, out_ref):
    frame_len = x_ref.shape[0] * 16
    ref_len = ref_ref.shape[0] * ref_ref.shape[3]
    groups = 16
    rows = groups * 16
    scale = LOG2E / math.sqrt(HD)
    nt = (((1,), (1,)), ((), ()))
    for slot in range(3):
        ab = 1 if slot == 2 else 0
        own_k = x_ref[:, 1, slot].reshape(frame_len, HD)
        own_v = x_ref[:, 2, slot].reshape(frame_len, HD)
        ref_k = ref_ref[:, 0, ab].reshape(ref_len, HD)
        ref_v = ref_ref[:, 1, ab].reshape(ref_len, HD)
        for block in range(x_ref.shape[0] // groups):
            at = slice(block * groups, (block + 1) * groups)
            query = x_ref[at, 0, slot].reshape(rows, HD)
            own = lax.dot_general(query, own_k, nt, preferred_element_type=jnp.float32)
            ref = lax.dot_general(query, ref_k, nt, preferred_element_type=jnp.float32)
            highest = jnp.maximum(
                jnp.max(own, axis=1, keepdims=True), jnp.max(ref, axis=1, keepdims=True)
            )
            own = jnp.exp2((own - highest) * scale)
            ref = jnp.exp2((ref - highest) * scale)
            totals = jnp.sum(own, axis=1, keepdims=True) + jnp.sum(ref, axis=1, keepdims=True)
            numerator = jnp.dot(
                own.astype(jnp.bfloat16), own_v, preferred_element_type=jnp.float32
            ) + jnp.dot(ref.astype(jnp.bfloat16), ref_v, preferred_element_type=jnp.float32)
            out_ref[at, slot] = (numerator / totals).astype(jnp.bfloat16).reshape(groups, 16, HD)


def call(kernel, out_shape, *args, flops=0):
    size = sum(a.size * 2 for a in args) + 2 * math.prod(out_shape)
    return pl.pallas_call(
        kernel,
        out_shape=jax.ShapeDtypeStruct(out_shape, jnp.bfloat16),
        in_specs=[VMEM] * len(args),
        out_specs=VMEM,
        compiler_params=pltpu.CompilerParams(vmem_limit_bytes=48 * 1024 * 1024),
        cost_estimate=pl.CostEstimate(flops=flops, bytes_accessed=size, transcendentals=0),
    )(*args)


def temporal_attention(query, key, value):
    scores = jnp.einsum("ftd,gtd->tfg", query, key, preferred_element_type=jnp.float32)
    scores = scores * (1.0 / math.sqrt(HD))
    highest = jnp.max(scores, axis=-1, keepdims=True)
    weights = jnp.exp(scores - highest)
    totals = jnp.sum(weights, axis=-1, keepdims=True)
    numerator = jnp.einsum(
        "tfg,gtd->ftd", weights.astype(jnp.bfloat16), value, preferred_element_type=jnp.float32
    )
    return (numerator / jnp.transpose(totals, (1, 0, 2))).astype(jnp.bfloat16)


def swap(tensor, mask):
    return lax.ppermute(tensor, ("zl0", "core"), [(i, i ^ mask) for i in range(4)])


def local(queries, keys, values, ref_keys, ref_values):
    core = lax.axis_index("core")
    quarter = lax.axis_index("zl0") * 2 + core

    refs = call(pack_refs_kernel, (16, 2, 2, 3, HD), ref_keys, ref_values)
    refs = lax.all_to_all(refs, Z, split_axis=0, concat_axis=0, tiled=True)
    packed = call(pack_kernel, (16, 4, 3, 3, 16, HD), queries, keys, values)
    refs, packed = lax.optimization_barrier((refs, packed))
    refs = refs.transpose(1, 2, 0, 3, 4).reshape(1, 2, 2, 48, HD)
    refs = lax.all_gather(refs, ("core", "y", "x"), axis=0, tiled=True)

    spread = lax.all_to_all(packed, Z, split_axis=0, concat_axis=0, tiled=True)
    spread = spread.reshape(4, 4, 4, 3, 3, 16, HD)

    by_frame = spread.transpose(0, 2, 1, 3, 4, 5, 6).reshape(16, 4, 3, 3, 16, HD)
    by_frame = lax.all_to_all(by_frame, YX, split_axis=0, concat_axis=0, tiled=True)
    by_frame = by_frame.reshape(64, 3, 3, 16, HD)
    spatial = call(
        spatial_kernel, (64, 3, 16, HD), by_frame, refs, flops=4 * 3 * 1024 * 2560 * HD
    )
    spatial = lax.all_to_all(
        spatial.reshape(16, 4, 3, 16, HD), YX, split_axis=0, concat_axis=0, tiled=True
    ).reshape(4, 4, 4, 3, 16, HD)

    first = spread[..., :2, :, :]
    mine = lax.dynamic_slice_in_dim(first, 2 * core, 2, axis=1)
    other = swap(lax.dynamic_slice_in_dim(first, 2 - 2 * core, 2, axis=1), 1)
    both = jnp.stack((mine, other))
    both = both.transpose(4, 0, 1, 3, 5, 2, 6, 7).reshape(3, 64, 32, HD)
    result = temporal_attention(both[0], both[1], both[2])
    result = result.reshape(2, 4, 4, 2, 2, 16, HD)
    mine, other = result[0], swap(result[1], 1)
    is_first = core == 0
    halves = (jnp.where(is_first, mine, other), jnp.where(is_first, other, mine))
    own_head = jnp.concatenate(halves, axis=3).transpose(0, 1, 3, 2, 4, 5)

    middle = spread[..., 2, :, :]
    parts = []
    for mask in range(4):
        part = lax.dynamic_index_in_dim(middle, quarter ^ mask, axis=1, keepdims=False)
        parts.append(swap(part, mask) if mask else part)
    four = jnp.stack(parts)
    four = four.transpose(3, 0, 1, 2, 4, 5).reshape(3, 64, 16, HD)
    result = temporal_attention(four[0], four[1], four[2]).reshape(4, 4, 4, 16, HD)
    parts = jnp.stack([swap(result[mask], mask) if mask else result[0] for mask in range(4)])
    middle_head = jnp.stack(
        [lax.dynamic_index_in_dim(parts, quarter ^ zh, axis=0, keepdims=False) for zh in range(4)],
        axis=2,
    )

    temporal = jnp.concatenate((own_head, middle_head[:, :, :, None]), axis=3)
    attended = (spatial.astype(jnp.float32) + temporal.astype(jnp.float32)).astype(jnp.bfloat16)
    attended = attended.transpose(0, 2, 1, 3, 4, 5).reshape(16, 4, 3, 16, HD)
    attended = lax.all_to_all(attended, Z, split_axis=0, concat_axis=0, tiled=True)
    return call(unpack_kernel, queries.shape, attended)


def solution(mesh):
    split = Mesh(mesh.devices.reshape(2, 2, 2, 4, 4, 4), ("zl1", "zl0", "core", "y", "zh", "x"))
    rows = P(("zl1", "zl0", "core"), ("y", "zh", "x"), None)
    refs = P(("zl1", "zl0", "core", "y", "zh", "x"), None)
    return jax.shard_map(
        local,
        mesh=split,
        in_specs=(rows, rows, rows, refs, refs),
        out_specs=rows,
        check_vma=False,
    )
```

```python
import math

import jax
import jax.numpy as jnp
from jax import lax
from jax.experimental import pallas as pl
from jax.experimental.pallas import tpu as pltpu
from jax.sharding import Mesh, PartitionSpec as P

HD = 128
LOG2E = 1.4426950408889634
Z = ("zl1", "zl0", "zh")
YX = ("y", "x")
VMEM = pl.BlockSpec(memory_space=pltpu.VMEM)
FIRST_ROWS = 4 * 3 * 16 + 16


def head_of(z_index, middle):
    zl1, zl0, zh = z_index // 8, (z_index // 4) % 2, z_index % 4
    pair = zh * 2 + zl1
    return pair * 3 + (1 if middle else 2 * zl0)


def frame_of(z_index, j, slot):
    zl0 = (z_index // 4) % 2
    return 4 * zl0 + j if slot == 2 else 2 * j + slot


def columns(head):
    return slice(head * HD, (head + 1) * HD)


def pack_first_kernel(q_ref, k_ref, v_ref, ref_key_ref, ref_value_ref, out_ref):
    for z in range(16):
        for j in range(4):
            for t, ref in enumerate((q_ref, k_ref, v_ref)):
                at = (j * 3 + t) * 16
                out_ref[z, at : at + 16] = ref[frame_of(z, j, 2), :, columns(head_of(z, True))]
        for t, ref in enumerate((ref_key_ref, ref_value_ref)):
            for middle in range(2):
                at = 192 + (t * 2 + middle) * 4
                out_ref[z, at : at + 3] = ref[:, columns(head_of(z, middle))]


def pack_second_kernel(q_ref, k_ref, v_ref, out_ref):
    for z in range(16):
        for j in range(4):
            for slot in range(2):
                for t, ref in enumerate((q_ref, k_ref, v_ref)):
                    out_ref[z, j, t, slot] = ref[frame_of(z, j, slot), :, columns(head_of(z, False))]


def split_first_kernel(in_ref, refs_ref, *frame_refs):
    y, x = lax.axis_index("y"), lax.axis_index("x")
    for z in range(16):
        for t in range(2):
            for middle in range(2):
                at = 192 + (t * 2 + middle) * 4
                refs_ref[0, t, middle, z * 3 : z * 3 + 3] = in_ref[z, at : at + 3]
    for k, frame_ref in enumerate(frame_refs):
        zl = lax.rem(y + k, 4)
        for m in range(4):
            j = lax.rem(x + m, 4)
            for zh in range(4):
                for t in range(3):
                    at = pl.multiple_of((j * 3 + t) * 16, 16)
                    frame_ref[m, zh, t] = in_ref[zl * 4 + zh, pl.ds(at, 16)]


def split_second_kernel(in_ref, first_ref, frame_ref, mine_ref, other_ref):
    core = lax.axis_index("core")
    for zl in range(4):
        for j in range(4):
            for zh in range(4):
                frame_ref[zl * 4 + j, zh] = in_ref[zl, zh, j]
            for half in range(2):
                for ref, zh in ((mine_ref, 2 * core + half), (other_ref, 2 - 2 * core + half)):
                    for t in range(3):
                        for slot in range(2):
                            ref[t, slot, zl * 4 + j, half] = in_ref[zl, zh, j, t, slot]
                        at = (j * 3 + t) * 16
                        ref[t, 2, zl * 4 + j, half] = first_ref[zl * 4 + zh, at : at + 16]


def attend(query, own_k, own_v, ref_k, ref_v):
    scale = LOG2E / math.sqrt(HD)
    nt = (((1,), (1,)), ((), ()))
    own = lax.dot_general(query, own_k, nt, preferred_element_type=jnp.float32)
    ref = lax.dot_general(query, ref_k, nt, preferred_element_type=jnp.float32)
    highest = jnp.maximum(jnp.max(own, axis=1, keepdims=True), jnp.max(ref, axis=1, keepdims=True))
    own = jnp.exp2((own - highest) * scale)
    ref = jnp.exp2((ref - highest) * scale)
    totals = jnp.sum(own, axis=1, keepdims=True) + jnp.sum(ref, axis=1, keepdims=True)
    numerator = jnp.dot(own.astype(jnp.bfloat16), own_v, preferred_element_type=jnp.float32)
    numerator += jnp.dot(ref.astype(jnp.bfloat16), ref_v, preferred_element_type=jnp.float32)
    return (numerator / totals).astype(jnp.bfloat16)


def spatial_first_kernel(*refs):
    *parts, ref_ref, out_ref = refs
    y, x = lax.axis_index("y"), lax.axis_index("x")
    own_k = jnp.concatenate([part[:, :, 1].reshape(256, HD) for part in parts])
    own_v = jnp.concatenate([part[:, :, 2].reshape(256, HD) for part in parts])
    ref_k = ref_ref[:, 0, 1].reshape(-1, HD)
    ref_v = ref_ref[:, 1, 1].reshape(-1, HD)
    for m, part in enumerate(parts):
        result = attend(part[:, :, 0].reshape(256, HD), own_k, own_v, ref_k, ref_v)
        result = result.reshape(4, 4, 16, HD)
        for k in range(4):
            out_ref[lax.rem(y + 4 - k, 4) * 4 + lax.rem(x + 4 - m, 4)] = result[k]


def spatial_second_kernel(x_ref, ref_ref, first_ref, out_ref):
    out_ref[:, :, 2] = first_ref[...]
    ref_k = ref_ref[:, 0, 0].reshape(-1, HD)
    ref_v = ref_ref[:, 1, 0].reshape(-1, HD)
    for slot in range(2):
        own_k = x_ref[:, :, 1, slot].reshape(1024, HD)
        own_v = x_ref[:, :, 2, slot].reshape(1024, HD)
        for block in range(4):
            at = slice(block * 4, block * 4 + 4)
            result = attend(x_ref[at, :, 0, slot].reshape(256, HD), own_k, own_v, ref_k, ref_v)
            out_ref[at, :, slot] = result.reshape(4, 4, 16, HD)


def sum_kernel(spatial_ref, mine_ref, other_ref, out_ref):
    core = lax.axis_index("core")
    for zl in range(4):
        for j in range(4):
            for half in range(2):
                for ref, first in ((mine_ref, 2 * core), (other_ref, 2 - 2 * core)):
                    zh = first + half
                    both = spatial_ref[zl * 4 + j, zh].astype(jnp.float32)
                    both += ref[:, zl * 4 + j, half].astype(jnp.float32)
                    out_ref[zl, zh, j] = both.astype(jnp.bfloat16)


def unpack_kernel(in_ref, out_ref):
    for z in range(16):
        for j in range(4):
            for slot in range(3):
                out_ref[frame_of(z, j, slot), :, columns(head_of(z, slot == 2))] = in_ref[z, j, slot]


def call(kernel, out_shapes, *args, flops=0):
    several = isinstance(out_shapes, list)
    shapes = [jax.ShapeDtypeStruct(s, jnp.bfloat16) for s in (out_shapes if several else [out_shapes])]
    size = sum(a.size * 2 for a in args) + sum(2 * math.prod(s.shape) for s in shapes)
    return pl.pallas_call(
        kernel,
        out_shape=shapes if several else shapes[0],
        in_specs=[VMEM] * len(args),
        out_specs=[VMEM] * len(shapes) if several else VMEM,
        compiler_params=pltpu.CompilerParams(vmem_limit_bytes=48 * 1024 * 1024),
        cost_estimate=pl.CostEstimate(flops=flops, bytes_accessed=size, transcendentals=0),
    )(*args)


def temporal_attention(query, key, value):
    scores = jnp.einsum("ftd,gtd->tfg", query, key, preferred_element_type=jnp.float32)
    scores = scores * (1.0 / math.sqrt(HD))
    highest = jnp.max(scores, axis=-1, keepdims=True)
    weights = jnp.exp(scores - highest)
    totals = jnp.sum(weights, axis=-1, keepdims=True)
    numerator = jnp.einsum(
        "tfg,gtd->ftd", weights.astype(jnp.bfloat16), value, preferred_element_type=jnp.float32
    )
    return (numerator / jnp.transpose(totals, (1, 0, 2))).astype(jnp.bfloat16)


def swap(tensor, mask):
    return lax.ppermute(tensor, ("zl0", "core"), [(i, i ^ mask) for i in range(4)])


def shift(tensor, axis, step):
    return lax.ppermute(tensor, axis, [(i, (i + step) % 4) for i in range(4)])


def gather_refs(refs):
    refs = jnp.concatenate((refs, lax.ppermute(refs, "core", [(0, 1), (1, 0)])))
    for axis in YX:
        refs = jnp.concatenate([refs] + [shift(refs, axis, step) for step in (1, 3, 2)])
    return refs


def local(queries, keys, values, ref_keys, ref_values):
    first = call(
        pack_first_kernel, (16, FIRST_ROWS, HD), queries, keys, values, ref_keys, ref_values
    )
    first = lax.all_to_all(first, Z, split_axis=0, concat_axis=0, tiled=True)
    second = call(pack_second_kernel, (16, 4, 3, 2, 16, HD), queries, keys, values)
    first, second = lax.optimization_barrier((first, second))
    second = lax.all_to_all(second, Z, split_axis=0, concat_axis=0, tiled=True)

    refs, *parts = call(
        split_first_kernel, [(1, 2, 2, 48, HD)] + [(4, 4, 3, 16, HD)] * 4, first
    )
    parts = [parts[0]] + [shift(parts[step], "y", step) for step in (1, 2, 3)]
    parts = [jnp.stack([part[m] for part in parts]) for m in range(4)]
    parts = [parts[0]] + [shift(parts[step], "x", step) for step in (1, 2, 3)]
    refs = gather_refs(refs)
    middle = call(
        spatial_first_kernel, (16, 4, 16, HD), *parts, refs, flops=4 * 1024 * 2560 * HD
    )

    second, middle, refs = lax.optimization_barrier((second, middle, refs))
    by_frame, mine, other = call(
        split_second_kernel,
        [(16, 4, 3, 2, 16, HD), (3, 3, 16, 2, 16, HD), (3, 3, 16, 2, 16, HD)],
        second.reshape(4, 4, 4, 3, 2, 16, HD),
        first,
    )

    by_frame = lax.all_to_all(by_frame, YX, split_axis=0, concat_axis=0, tiled=True)
    spatial = call(
        spatial_second_kernel,
        (16, 4, 3, 16, HD),
        by_frame,
        refs,
        middle,
        flops=8 * 1024 * 2560 * HD,
    )
    spatial = lax.all_to_all(spatial, YX, split_axis=0, concat_axis=0, tiled=True)

    got = swap(other, 1)
    own_head = jnp.stack((mine[:, :2], got[:, :2]), axis=1).reshape(3, 64, 32, HD)
    own_head = temporal_attention(own_head[0], own_head[1], own_head[2])
    own_head = own_head.reshape(2, 2, 16, 2, 16, HD)
    zl0 = lax.axis_index("zl0")
    middle = jnp.stack((mine[:, 2], got[:, 2]), axis=1)
    send = lax.dynamic_index_in_dim(middle, 1 - zl0, axis=3, keepdims=False)
    keep = lax.dynamic_index_in_dim(middle, zl0, axis=3, keepdims=False)
    middle = jnp.stack((keep, swap(send, 2)), axis=1).reshape(3, 64, 16, HD)
    middle = temporal_attention(middle[0], middle[1], middle[2])
    keep, send = middle[:32], middle[32:]
    got = swap(send, 2)
    middle = jnp.stack(
        (jnp.where(zl0 == 0, keep, got), jnp.where(zl0 == 0, got, keep)), axis=1
    ).reshape(2, 1, 16, 2, 16, HD)
    temporal = jnp.concatenate((own_head, middle), axis=1)
    mine, other = temporal[0], swap(temporal[1], 1)

    attended = call(sum_kernel, (4, 4, 4, 3, 16, HD), spatial, mine, other)
    attended = attended.reshape(16, 4, 3, 16, HD)
    attended = lax.all_to_all(attended, Z, split_axis=0, concat_axis=0, tiled=True)
    return call(unpack_kernel, queries.shape, attended)


def solution(mesh):
    split = Mesh(mesh.devices.reshape(2, 2, 2, 4, 4, 4), ("zl1", "zl0", "core", "y", "zh", "x"))
    rows = P(("zl1", "zl0", "core"), ("y", "zh", "x"), None)
    refs = P(("zl1", "zl0", "core", "y", "zh", "x"), None)
    return jax.shard_map(
        local,
        mesh=split,
        in_specs=(rows, rows, rows, refs, refs),
        out_specs=rows,
        check_vma=False,
    )
```

```python
import math

import jax
import jax.numpy as jnp
from jax import lax
from jax.experimental import pallas as pl
from jax.experimental.pallas import tpu as pltpu
from jax.sharding import Mesh, PartitionSpec as P

HD = 128
LOG2E = 1.4426950408889634
Z = ("zl1", "zl0", "zh")
YX = ("y", "x")
VMEM = pl.BlockSpec(memory_space=pltpu.VMEM)
HBM = pl.BlockSpec(memory_space=pltpu.HBM)


def head_of(z_index, middle):
    zl1, zl0, zh = z_index // 8, (z_index // 4) % 2, z_index % 4
    pair = zh * 2 + zl1
    return pair * 3 + (1 if middle else 2 * zl0)


def frame_of(z_index, j, slot):
    zl0 = (z_index // 4) % 2
    return 4 * zl0 + j if slot == 2 else 2 * j + slot


def columns(head):
    return slice(head * HD, (head + 1) * HD)


def pack_first_kernel(q_ref, k_ref, v_ref, ref_key_ref, ref_value_ref, out_ref, key_rows, value_rows, sems):
    copies = [
        pltpu.make_async_copy(ref_key_ref, key_rows, sems.at[48]),
        pltpu.make_async_copy(ref_value_ref, value_rows, sems.at[49]),
    ]
    for z in range(16):
        for t, ref in enumerate((q_ref, k_ref, v_ref)):
            frames = pl.ds(frame_of(z, 0, 2), 4)
            source = ref.at[frames, :, pl.ds(head_of(z, True) * HD, HD)]
            target = out_ref.at[z, pl.ds(t * 4, 4)]
            copies.append(pltpu.make_async_copy(source, target, sems.at[z * 3 + t]))
    for copy in copies:
        copy.start()
    for copy in copies[:2]:
        copy.wait()
    for z in range(16):
        for t, ref in enumerate((key_rows, value_rows)):
            for middle in range(2):
                at = (t * 2 + middle) * 4
                out_ref[z, 12, at : at + 3] = ref[:, columns(head_of(z, middle))]
    for copy in copies[2:]:
        copy.wait()


def pack_second_kernel(q_ref, k_ref, v_ref, out_ref):
    for z in range(16):
        for j in range(4):
            for slot in range(2):
                for t, ref in enumerate((q_ref, k_ref, v_ref)):
                    out_ref[z, j, t, slot] = ref[frame_of(z, j, slot), :, columns(head_of(z, False))]


def split_first_kernel(in_ref, *outs):
    *part_refs, other_ref, rows_ref = outs
    y, x, core = lax.axis_index("y"), lax.axis_index("x"), lax.axis_index("core")
    for zl in range(4):
        for half in range(2):
            other_ref[zl, half] = in_ref[zl * 4 + 2 - 2 * core + half, :12]
    for z in range(16):
        for t in range(2):
            for middle in range(2):
                at = (t * 2 + middle) * 4
                rows_ref[t, middle, z * 3 : z * 3 + 3] = in_ref[z, 12, at : at + 3]
    rows = rows_ref[...].reshape(12, 16, HD)
    for k, part_ref in enumerate(part_refs):
        zl = lax.rem(y + k, 4)
        for m in range(4):
            j = lax.rem(x + m, 4)
            for zh in range(4):
                for t in range(3):
                    part_ref[m, zh * 3 + t] = in_ref[zl * 4 + zh, t * 4 + j]
        part_ref[4] = rows


def send_kernel(first_ref, got_ref, out_ref):
    core, half = lax.axis_index("core"), 1 - lax.axis_index("zl0")
    for zl in range(4):
        out_ref[0, zl] = first_ref[zl * 4 + 2 * core + half, :12]
        out_ref[1, zl] = got_ref[zl, half]


def split_second_kernel(in_ref, frame_ref):
    for zl in range(4):
        for zh in range(4):
            for j in range(4):
                frame_ref[zl * 4 + j, zh] = in_ref[zl, zh, j]


def other_kernel(in_ref, other_ref):
    core = lax.axis_index("core")
    for zl in range(4):
        for half in range(2):
            other_ref[zl, half] = in_ref[zl, 2 - 2 * core + half]


def token_bias(bias_ref):
    rows = lax.broadcasted_iota(jnp.int32, bias_ref.shape, 0)
    columns = lax.broadcasted_iota(jnp.int32, bias_ref.shape, 1)
    bias_ref[...] = jnp.where(((rows ^ columns) & 15) == 0, 0.0, -1e30)


def attend_tokens(queries, keys, values, bias_ref):
    scale = LOG2E / math.sqrt(HD)
    key, value = jnp.concatenate(keys), jnp.concatenate(values)
    for query in queries:
        scores = lax.dot_general(
            query, key, (((1,), (1,)), ((), ())), preferred_element_type=jnp.float32
        )
        scores += bias_ref[...]
        highest = jnp.max(scores, axis=1, keepdims=True)
        weights = jnp.exp2((scores - highest) * scale)
        totals = jnp.sum(weights, axis=1, keepdims=True)
        result = jnp.dot(weights.astype(jnp.bfloat16), value, preferred_element_type=jnp.float32)
        yield (result / totals).astype(jnp.bfloat16).reshape(16, 16, HD)


def temporal_middle_kernel(first_ref, got_ref, recv_ref, keep_ref, send_ref, bias_ref):
    core, half = lax.axis_index("core"), lax.axis_index("zl0")
    token_bias(bias_ref)

    def block(part, t):
        at = slice(t * 4, t * 4 + 4)
        if part == 0:
            tiles = [first_ref[zl * 4 + 2 * core + half, at] for zl in range(4)]
        elif part == 1:
            tiles = [got_ref[zl, half, at] for zl in range(4)]
        else:
            tiles = [recv_ref[part - 2, zl, at] for zl in range(4)]
        return jnp.concatenate(tiles).reshape(256, HD)

    tensors = [[block(part, t) for part in range(4)] for t in range(3)]
    for part, result in enumerate(attend_tokens(*tensors, bias_ref)):
        (keep_ref if part < 2 else send_ref)[part % 2] = result


def temporal_own_kernel(in_ref, got_ref, mine_ref, other_ref, bias_ref):
    core = lax.axis_index("core")
    token_bias(bias_ref)
    for half in range(2):

        def block(part, slot, t):
            if part == 0:
                tiles = [in_ref[zl, 2 * core + half, :, t * 2 + slot] for zl in range(4)]
            else:
                tiles = [got_ref[zl, half, :, t * 2 + slot] for zl in range(4)]
            return jnp.concatenate(tiles).reshape(256, HD)

        blocks = [(part, slot) for part in range(2) for slot in range(2)]
        tensors = [[block(part, slot, t) for part, slot in blocks] for t in range(3)]
        for (part, slot), result in zip(blocks, attend_tokens(*tensors, bias_ref)):
            (other_ref if part else mine_ref)[slot, :, half] = result


def attend(query, own_k, ref_k, values):
    scale = LOG2E / math.sqrt(HD)
    nt = (((1,), (1,)), ((), ()))
    own = lax.dot_general(query, own_k, nt, preferred_element_type=jnp.float32)
    ref = lax.dot_general(query, ref_k, nt, preferred_element_type=jnp.float32)
    highest = jnp.maximum(jnp.max(own, axis=1, keepdims=True), jnp.max(ref, axis=1, keepdims=True))
    own = jnp.exp2((own - highest) * scale).astype(jnp.bfloat16)
    ref = jnp.exp2((ref - highest) * scale).astype(jnp.bfloat16)
    own_v, ref_v = values()
    result = jnp.dot(own, own_v, preferred_element_type=jnp.float32)
    result += jnp.dot(ref, ref_v, preferred_element_type=jnp.float32)
    return (result[:, :HD] / result[:, HD:]).astype(jnp.bfloat16)


def with_ones(value):
    return jnp.concatenate((value, jnp.ones_like(value)), axis=1)


def ref_rows(mine_ref, other_ref, t, middle):
    at = t * 6 + middle * 3
    parts = [ref[:, :, at : at + 3].reshape(768, HD) for ref in (mine_ref, other_ref)]
    return jnp.concatenate(parts)


def spatial_first_kernel(*refs):
    *parts, mine_ref, other_ref, out_ref = refs
    y, x = lax.axis_index("y"), lax.axis_index("x")

    def tensor(part, t):
        return jnp.stack([part[0, :, zh * 3 + t] for zh in range(4)], axis=1).reshape(256, HD)

    own_k = jnp.concatenate([tensor(part, 1) for part in parts])
    own_v = with_ones(jnp.concatenate([tensor(part, 2) for part in parts]))
    ref_k = ref_rows(mine_ref, other_ref, 0, 1)
    ref_v = with_ones(ref_rows(mine_ref, other_ref, 1, 1))
    for m, part in enumerate(parts):
        result = attend(tensor(part, 0), own_k, ref_k, lambda: (own_v, ref_v))
        result = result.reshape(4, 4, 16, HD)
        for k in range(4):
            out_ref[lax.rem(y + 4 - k, 4) * 4 + lax.rem(x + 4 - m, 4)] = result[k]


def spatial_second_kernel(x_hbm, mine_hbm, other_hbm, first_hbm, out_ref, x_ref, mine_ref, other_ref, sems):
    moves = [(first_hbm, out_ref.at[:, :, 2])]
    for start, blocks, source, target in (
        (0, 4, x_hbm, x_ref),
        (0, 3, mine_hbm, mine_ref),
        (0, 3, other_hbm, other_ref),
        (4, 2, x_hbm, x_ref),
        (6, 3, mine_hbm, mine_ref),
        (6, 3, other_hbm, other_ref),
    ):
        at = pl.ds(start, blocks)
        moves.append((source.at[:, :, at], target.at[:, :, at]))
    passed, *copies = [pltpu.make_async_copy(*move, sems.at[i]) for i, move in enumerate(moves)]
    for copy in copies:
        copy.start()
    passed.start()
    for copy in copies[:3]:
        copy.wait()
    ref_k = ref_rows(mine_ref, other_ref, 0, 0)
    held = {}

    def values(slot):
        if not held:
            for copy in copies[3:]:
                copy.wait()
            held["ref"] = with_ones(ref_rows(mine_ref, other_ref, 1, 0))
        if slot not in held:
            held[slot] = with_ones(x_ref[:, :, 4 + slot].reshape(1024, HD))
        return held[slot], held["ref"]

    for slot in range(2):
        own_k = x_ref[:, :, 2 + slot].reshape(1024, HD)
        for block in range(4):
            at = slice(block * 4, block * 4 + 4)
            query = x_ref[at, :, slot].reshape(256, HD)
            result = attend(query, own_k, ref_k, lambda: values(slot))
            out_ref[at, :, slot] = result.reshape(4, 4, 16, HD)
    passed.wait()


def sum_kernel(spatial_ref, mine_ref, other_ref, keep_ref, back_ref, middle_ref, out_ref):
    core, zl0 = lax.axis_index("core"), lax.axis_index("zl0")

    def add(group, zh, slot, temporal):
        both = spatial_ref[group, zh, slot].astype(jnp.float32) + temporal.astype(jnp.float32)
        out_ref[group // 4, zh, group % 4, slot] = both.astype(jnp.bfloat16)

    for group in range(16):
        for half in range(2):
            for slot in range(2):
                add(group, 2 * core + half, slot, mine_ref[slot, group, half])
                add(group, 2 - 2 * core + half, slot, other_ref[slot, group, half])
        add(group, 2 * core + zl0, 2, keep_ref[0, group])
        add(group, 2 * core + 1 - zl0, 2, back_ref[0, group])
        add(group, 2 - 2 * core + zl0, 2, middle_ref[0, group])
        add(group, 2 - 2 * core + 1 - zl0, 2, middle_ref[1, group])


def unpack_kernel(in_ref, out_ref):
    for z in range(16):
        for j in range(4):
            for slot in range(3):
                out_ref[frame_of(z, j, slot), :, columns(head_of(z, slot == 2))] = in_ref[z, j, slot]


def call(kernel, out_shapes, *args, flops=0, scratch=(), in_spec=VMEM, vmem=32):
    several = isinstance(out_shapes, list)
    shapes = [jax.ShapeDtypeStruct(s, jnp.bfloat16) for s in (out_shapes if several else [out_shapes])]
    size = sum(a.size * 2 for a in args) + sum(2 * math.prod(s.shape) for s in shapes)
    cost = pl.CostEstimate(flops=flops, bytes_accessed=size, transcendentals=0)
    return pl.pallas_call(
        kernel,
        out_shape=shapes if several else shapes[0],
        in_specs=[in_spec] * len(args),
        out_specs=[VMEM] * len(shapes) if several else VMEM,
        scratch_shapes=scratch,
        compiler_params=pltpu.CompilerParams(vmem_limit_bytes=vmem * 1024 * 1024),
        cost_estimate=cost,
    )(*args)


def swap(tensor, mask):
    return lax.ppermute(tensor, ("zl0", "core"), [(i, i ^ mask) for i in range(4)])


def shift(tensor, axis, step):
    return lax.ppermute(tensor, axis, [(i, (i + step) % 4) for i in range(4)])


def local(queries, keys, values, ref_keys, ref_values):
    first = call(
        pack_first_kernel,
        (16, 13, 16, HD),
        queries,
        keys,
        values,
        ref_keys,
        ref_values,
        in_spec=HBM,
        vmem=62,
        scratch=[
            pltpu.VMEM(ref_keys.shape, jnp.bfloat16),
            pltpu.VMEM(ref_keys.shape, jnp.bfloat16),
            pltpu.SemaphoreType.DMA((50,)),
        ],
    )
    first = lax.all_to_all(first, Z, split_axis=0, concat_axis=0, tiled=True)
    second = call(pack_second_kernel, (16, 4, 3, 2, 16, HD), queries, keys, values)
    first, second = lax.optimization_barrier((first, second))
    second = lax.all_to_all(second, Z, split_axis=0, concat_axis=0, tiled=True)

    *parts, other = call(
        split_first_kernel,
        [(5, 12, 16, HD)] * 4 + [(4, 2, 12, 16, HD)],
        first,
        scratch=[pltpu.VMEM((2, 2, 48, HD), jnp.bfloat16)],
    )
    parts = [parts[0]] + [shift(parts[step], "y", step) for step in (1, 2, 3)]
    rows = [part[4] for part in parts]
    parts = [jnp.stack([part[m] for part in parts] + rows).reshape(2, 4, 12, 16, HD) for m in range(4)]
    parts = [parts[0]] + [shift(parts[step], "x", step) for step in (1, 2, 3)]
    my_refs = jnp.stack([part[1] for part in parts])
    refs = (my_refs, lax.ppermute(my_refs, "core", [(0, 1), (1, 0)]))
    middle = call(
        spatial_first_kernel, (16, 4, 16, HD), *parts, *refs, flops=4 * 1024 * 2560 * HD
    )
    got = swap(other, 1)

    send = call(send_kernel, (2, 4, 12, 16, HD), first, got)

    second, middle, refs, send = lax.optimization_barrier((second, middle, refs, send))
    second = second.reshape(4, 4, 4, 6, 16, HD)
    by_frame = call(split_second_kernel, (16, 4, 6, 16, HD), second)
    other = call(other_kernel, (4, 2, 4, 6, 16, HD), second)

    by_frame = lax.all_to_all(by_frame, YX, split_axis=0, concat_axis=0, tiled=True)

    bias = [pltpu.VMEM((256, 1024), jnp.float32)]
    mine, other = call(
        temporal_own_kernel, [(2, 16, 2, 16, HD)] * 2, second, swap(other, 1), scratch=bias
    )
    recv, mine, other = lax.optimization_barrier((swap(send, 2), mine, other))
    keep, send = call(
        temporal_middle_kernel, [(2, 16, 16, HD)] * 2, first, got, recv, scratch=bias
    )
    by_frame, other, send = lax.optimization_barrier((by_frame, other, send))
    back = swap(send, 2)
    other = swap(other, 1)
    middle_other = swap(jnp.stack((keep[1], back[1])), 1)

    spatial = call(
        spatial_second_kernel,
        (16, 4, 3, 16, HD),
        by_frame,
        *refs,
        middle,
        flops=8 * 1024 * 2560 * HD,
        in_spec=HBM,
        vmem=62,
        scratch=[
            pltpu.VMEM((16, 4, 6, 16, HD), jnp.bfloat16),
            pltpu.VMEM((4, 4, 12, 16, HD), jnp.bfloat16),
            pltpu.VMEM((4, 4, 12, 16, HD), jnp.bfloat16),
            pltpu.SemaphoreType.DMA((7,)),
        ],
    )
    spatial = lax.all_to_all(spatial, YX, split_axis=0, concat_axis=0, tiled=True)

    attended = call(
        sum_kernel, (4, 4, 4, 3, 16, HD), spatial, mine, other, keep, back, middle_other
    )
    attended = attended.reshape(16, 4, 3, 16, HD)
    attended = lax.all_to_all(attended, Z, split_axis=0, concat_axis=0, tiled=True)
    return call(unpack_kernel, queries.shape, attended)


def solution(mesh):
    split = Mesh(mesh.devices.reshape(2, 2, 2, 4, 4, 4), ("zl1", "zl0", "core", "y", "zh", "x"))
    rows = P(("zl1", "zl0", "core"), ("y", "zh", "x"), None)
    refs = P(("zl1", "zl0", "core", "y", "zh", "x"), None)
    return jax.shard_map(
        local,
        mesh=split,
        in_specs=(rows, rows, rows, refs, refs),
        out_specs=rows,
        check_vma=False,
    )
```

```python
import math

import jax
import jax.numpy as jnp
from jax import lax
from jax.experimental import pallas as pl
from jax.experimental.pallas import tpu as pltpu
from jax.sharding import Mesh, PartitionSpec as P

HD = 128
LOG2E = 1.4426950408889634
Z = ("zh1", "zl1", "zl0", "zh0")
YX = ("y", "x")
VMEM = pl.BlockSpec(memory_space=pltpu.VMEM)
HBM = pl.BlockSpec(memory_space=pltpu.HBM)


def z_index(zl, zh1, zh0):
    at = {"zl1": zl // 2, "zl0": zl % 2, "zh1": zh1, "zh0": zh0}
    return at[Z[0]] * 8 + at[Z[1]] * 4 + at[Z[2]] * 2 + at[Z[3]]


def chip_of(index):
    at = {axis: index >> (3 - i) & 1 for i, axis in enumerate(Z)}
    return at["zl1"], at["zl0"], at["zh1"] * 2 + at["zh0"]


def head_of(index, middle):
    zl1, zl0, zh = chip_of(index)
    return (zh * 2 + zl1) * 3 + (1 if middle else 2 * zl0)


def frame_of(index, j, slot):
    return 4 * chip_of(index)[1] + j if slot == 2 else 2 * j + slot


def columns(head):
    return slice(head * HD, (head + 1) * HD)


def pack_first_kernel(q_ref, k_ref, v_ref, ref_key_ref, ref_value_ref, out_hbm, out_ref, key_rows, value_rows, sems):
    rows = [
        pltpu.make_async_copy(ref_key_ref, key_rows, sems.at[64]),
        pltpu.make_async_copy(ref_value_ref, value_rows, sems.at[65]),
    ]
    reads, writes = [], []
    for z in range(16):
        for t, ref in enumerate((q_ref, k_ref, v_ref)):
            frames = pl.ds(frame_of(z, 0, 2), 4)
            source = ref.at[frames, :, pl.ds(head_of(z, True) * HD, HD)]
            target = out_ref.at[z, pl.ds(t * 4, 4)]
            reads.append(pltpu.make_async_copy(source, target, sems.at[z * 4 + t]))
        writes.append(pltpu.make_async_copy(out_ref.at[z], out_hbm.at[z], sems.at[z * 4 + 3]))
    for copy in rows + reads:
        copy.start()
    for copy in rows:
        copy.wait()
    for z in range(16):
        for t, ref in enumerate((key_rows, value_rows)):
            for middle in range(2):
                at = (t * 2 + middle) * 4
                out_ref[z, 12, at : at + 3] = ref[:, columns(head_of(z, middle))]
        for copy in reads[z * 3 : z * 3 + 3]:
            copy.wait()
        writes[z].start()
    for copy in writes:
        copy.wait()


def pack_second_kernel(q_ref, k_ref, v_ref, out_ref):
    for z in range(16):
        for j in range(4):
            for slot in range(2):
                for t, ref in enumerate((q_ref, k_ref, v_ref)):
                    out_ref[z, j, t, slot] = ref[frame_of(z, j, slot), :, columns(head_of(z, False))]


def split_first_kernel(in_ref, *outs):
    *part_refs, other_ref, rows_ref = outs
    y, x, core = lax.axis_index("y"), lax.axis_index("x"), lax.axis_index("core")
    for zl in range(4):
        for half in range(2):
            other_ref[zl, half] = in_ref[z_index(zl, 1 - core, half), :12]
    for z in range(16):
        for t in range(2):
            for middle in range(2):
                at = (t * 2 + middle) * 4
                rows_ref[t, middle, z * 3 : z * 3 + 3] = in_ref[z, 12, at : at + 3]
    rows = rows_ref[...].reshape(12, 16, HD)
    for k, part_ref in enumerate(part_refs):
        zl = lax.rem(y + k, 4)
        for m in range(4):
            j = lax.rem(x + m, 4)
            for zh in range(4):
                for t in range(3):
                    part_ref[m, zh * 3 + t] = in_ref[z_index(zl, zh // 2, zh % 2), t * 4 + j]
        part_ref[4] = rows


def send_kernel(first_ref, got_ref, out_ref):
    core, half = lax.axis_index("core"), 1 - lax.axis_index("zl0")
    for zl in range(4):
        out_ref[0, zl] = first_ref[z_index(zl, core, half), :12]
        out_ref[1, zl] = got_ref[zl, half]


def split_second_kernel(in_ref, frame_ref):
    for zl in range(4):
        for zh in range(4):
            for j in range(4):
                frame_ref[zl * 4 + j, zh] = in_ref[z_index(zl, zh // 2, zh % 2), j]


def other_kernel(in_ref, other_ref):
    core = lax.axis_index("core")
    for zl in range(4):
        for half in range(2):
            other_ref[zl, half] = in_ref[z_index(zl, 1 - core, half)]


def token_bias(bias_ref):
    rows = lax.broadcasted_iota(jnp.int32, bias_ref.shape, 0)
    columns = lax.broadcasted_iota(jnp.int32, bias_ref.shape, 1)
    bias_ref[...] = jnp.where(((rows ^ columns) & 15) == 0, 0.0, -1e30)


def attend_tokens(queries, keys, values, bias_ref):
    scale = LOG2E / math.sqrt(HD)
    key, value = jnp.concatenate(keys), jnp.concatenate(values)
    for query in queries:
        scores = lax.dot_general(
            query, key, (((1,), (1,)), ((), ())), preferred_element_type=jnp.float32
        )
        scores += bias_ref[...]
        highest = jnp.max(scores, axis=1, keepdims=True)
        weights = jnp.exp2((scores - highest) * scale)
        totals = jnp.sum(weights, axis=1, keepdims=True)
        result = jnp.dot(weights.astype(jnp.bfloat16), value, preferred_element_type=jnp.float32)
        yield (result / totals).astype(jnp.bfloat16).reshape(16, 16, HD)


def temporal_middle_kernel(first_ref, got_ref, recv_ref, keep_ref, send_ref, bias_ref):
    core, half = lax.axis_index("core"), lax.axis_index("zl0")
    token_bias(bias_ref)

    def block(part, t):
        at = slice(t * 4, t * 4 + 4)
        if part == 0:
            tiles = [first_ref[z_index(zl, core, half), at] for zl in range(4)]
        elif part == 1:
            tiles = [got_ref[zl, half, at] for zl in range(4)]
        else:
            tiles = [recv_ref[part - 2, zl, at] for zl in range(4)]
        return jnp.concatenate(tiles).reshape(256, HD)

    tensors = [[block(part, t) for part in range(4)] for t in range(3)]
    for part, result in enumerate(attend_tokens(*tensors, bias_ref)):
        (keep_ref if part < 2 else send_ref)[part % 2] = result


def temporal_own_kernel(in_ref, got_ref, mine_ref, other_ref, bias_ref):
    core = lax.axis_index("core")
    token_bias(bias_ref)
    for half in range(2):

        def block(part, slot, t):
            if part == 0:
                tiles = [in_ref[z_index(zl, core, half), :, t * 2 + slot] for zl in range(4)]
            else:
                tiles = [got_ref[zl, half, :, t * 2 + slot] for zl in range(4)]
            return jnp.concatenate(tiles).reshape(256, HD)

        blocks = [(part, slot) for part in range(2) for slot in range(2)]
        tensors = [[block(part, slot, t) for part, slot in blocks] for t in range(3)]
        for (part, slot), result in zip(blocks, attend_tokens(*tensors, bias_ref)):
            (other_ref if part else mine_ref)[slot, :, half] = result


def score(query, keys):
    nt = (((1,), (1,)), ((), ()))
    return [lax.dot_general(query, key, nt, preferred_element_type=jnp.float32) for key in keys]


def weigh(scores, values):
    scale = LOG2E / math.sqrt(HD)
    highest = [jnp.max(part, axis=1, keepdims=True) for part in scores]
    highest = jnp.maximum(*highest)
    weights = [jnp.exp2((part - highest) * scale).astype(jnp.bfloat16) for part in scores]
    result = [
        jnp.dot(part, value, preferred_element_type=jnp.float32)
        for part, value in zip(weights, values)
    ]
    result = result[0] + result[1]
    return (result[:, :HD] / result[:, HD:]).astype(jnp.bfloat16)


def with_ones(value):
    return jnp.concatenate((value, jnp.ones_like(value)), axis=1)


def ref_rows(mine_ref, other_ref, t, middle):
    at = t * 6 + middle * 3
    parts = [ref[:, :, at : at + 3].reshape(768, HD) for ref in (mine_ref, other_ref)]
    return jnp.concatenate(parts)


def spatial_first_kernel(*refs):
    *parts, mine_ref, other_ref, out_ref = refs
    y, x = lax.axis_index("y"), lax.axis_index("x")

    def tensor(part, t):
        return jnp.stack([part[0, :, zh * 3 + t] for zh in range(4)], axis=1).reshape(256, HD)

    own_k = jnp.concatenate([tensor(part, 1) for part in parts])
    own_v = with_ones(jnp.concatenate([tensor(part, 2) for part in parts]))
    keys = own_k, ref_rows(mine_ref, other_ref, 0, 1)
    values = own_v, with_ones(ref_rows(mine_ref, other_ref, 1, 1))
    for m, part in enumerate(parts):
        result = weigh(score(tensor(part, 0), keys), values)
        result = result.reshape(4, 4, 16, HD)
        for k in range(4):
            out_ref[lax.rem(y + 4 - k, 4) * 4 + lax.rem(x + 4 - m, 4)] = result[k]


def spatial_second_kernel(x_hbm, mine_hbm, other_hbm, first_hbm, out_hbm, x_ref, mine_ref, other_ref, out_ref, sems):
    moves = [(first_hbm, out_ref.at[2])]
    for start, blocks, source, target in (
        (0, 4, x_hbm, x_ref),
        (0, 3, mine_hbm, mine_ref),
        (0, 3, other_hbm, other_ref),
        (4, 2, x_hbm, x_ref),
        (6, 3, mine_hbm, mine_ref),
        (6, 3, other_hbm, other_ref),
    ):
        at = pl.ds(start, blocks)
        moves.append((source.at[:, :, at], target.at[:, :, at]))
    passed, *copies = [pltpu.make_async_copy(*move, sems.at[i]) for i, move in enumerate(moves)]
    for copy in copies:
        copy.start()
    passed.start()
    for copy in copies[:3]:
        copy.wait()
    ref_k = ref_rows(mine_ref, other_ref, 0, 0)
    blocks = [(slot, slice(at, at + 4)) for slot in range(2) for at in range(0, 16, 4)]

    def scores(slot, at):
        keys = x_ref[:, :, 2 + slot].reshape(1024, HD), ref_k
        return score(x_ref[at, :, slot].reshape(256, HD), keys)

    later = scores(*blocks[0])
    for copy in copies[3:]:
        copy.wait()
    ref_v = with_ones(ref_rows(mine_ref, other_ref, 1, 0))
    passed.wait()
    writes = [pltpu.make_async_copy(out_ref.at[2], out_hbm.at[:, :, 2], sems.at[15])]
    writes[0].start()
    for i, (slot, at) in enumerate(blocks):
        now, later = later, scores(*blocks[i + 1]) if i < 7 else None
        result = weigh(now, (with_ones(x_ref[:, :, 4 + slot].reshape(1024, HD)), ref_v))
        out_ref[slot, at] = result.reshape(4, 4, 16, HD)
        target = out_hbm.at[pl.ds(at.start, 4), :, slot]
        writes.append(pltpu.make_async_copy(out_ref.at[slot, pl.ds(at.start, 4)], target, sems.at[7 + i]))
        writes[-1].start()
    for write in writes:
        write.wait()


def sum_kernel(spatial_ref, mine_ref, other_ref, keep_ref, back_ref, middle_ref, out_ref):
    core, zl0 = lax.axis_index("core"), lax.axis_index("zl0")

    def add(group, zh1, zh0, slot, temporal):
        both = spatial_ref[group, zh1 * 2 + zh0, slot].astype(jnp.float32) + temporal.astype(jnp.float32)
        out_ref[z_index(group // 4, zh1, zh0), group % 4, slot] = both.astype(jnp.bfloat16)

    for group in range(16):
        for half in range(2):
            for slot in range(2):
                add(group, core, half, slot, mine_ref[slot, group, half])
                add(group, 1 - core, half, slot, other_ref[slot, group, half])
        add(group, core, zl0, 2, keep_ref[0, group])
        add(group, core, 1 - zl0, 2, back_ref[0, group])
        add(group, 1 - core, zl0, 2, middle_ref[0, group])
        add(group, 1 - core, 1 - zl0, 2, middle_ref[1, group])


def unpack_kernel(in_ref, out_ref):
    for z in range(16):
        for j in range(4):
            for slot in range(3):
                out_ref[frame_of(z, j, slot), :, columns(head_of(z, slot == 2))] = in_ref[z, j, slot]


def call(kernel, out_shapes, *args, flops=0, scratch=(), in_spec=VMEM, out_spec=VMEM, vmem=32):
    several = isinstance(out_shapes, list)
    shapes = [jax.ShapeDtypeStruct(s, jnp.bfloat16) for s in (out_shapes if several else [out_shapes])]
    size = sum(a.size * 2 for a in args) + sum(2 * math.prod(s.shape) for s in shapes)
    cost = pl.CostEstimate(flops=flops, bytes_accessed=size, transcendentals=0)
    return pl.pallas_call(
        kernel,
        out_shape=shapes if several else shapes[0],
        in_specs=[in_spec] * len(args),
        out_specs=[VMEM] * len(shapes) if several else out_spec,
        scratch_shapes=scratch,
        compiler_params=pltpu.CompilerParams(vmem_limit_bytes=vmem * 1024 * 1024),
        cost_estimate=cost,
    )(*args)


def swap(tensor, mask):
    return lax.ppermute(tensor, ("zl0", "core"), [(i, i ^ mask) for i in range(4)])


def shift(tensor, axis, step):
    return lax.ppermute(tensor, axis, [(i, (i + step) % 4) for i in range(4)])


def local(queries, keys, values, ref_keys, ref_values):
    first = call(
        pack_first_kernel,
        (16, 13, 16, HD),
        queries,
        keys,
        values,
        ref_keys,
        ref_values,
        in_spec=HBM,
        out_spec=HBM,
        vmem=62,
        scratch=[
            pltpu.VMEM((16, 13, 16, HD), jnp.bfloat16),
            pltpu.VMEM(ref_keys.shape, jnp.bfloat16),
            pltpu.VMEM(ref_keys.shape, jnp.bfloat16),
            pltpu.SemaphoreType.DMA((66,)),
        ],
    )
    first = lax.all_to_all(first, Z, split_axis=0, concat_axis=0, tiled=True)
    second = call(pack_second_kernel, (16, 4, 3, 2, 16, HD), queries, keys, values)
    first, second = lax.optimization_barrier((first, second))
    second = lax.all_to_all(second, Z, split_axis=0, concat_axis=0, tiled=True)

    *parts, other = call(
        split_first_kernel,
        [(5, 12, 16, HD)] * 4 + [(4, 2, 12, 16, HD)],
        first,
        scratch=[pltpu.VMEM((2, 2, 48, HD), jnp.bfloat16)],
    )
    parts = [parts[0]] + [shift(parts[step], "y", step) for step in (1, 2, 3)]
    rows = [part[4] for part in parts]
    parts = [jnp.stack([part[m] for part in parts] + rows).reshape(2, 4, 12, 16, HD) for m in range(4)]
    parts = [parts[0]] + [shift(parts[step], "x", step) for step in (1, 2, 3)]
    my_refs = jnp.stack([part[1] for part in parts])
    refs = (my_refs, lax.ppermute(my_refs, "core", [(0, 1), (1, 0)]))
    middle = call(
        spatial_first_kernel, (16, 4, 16, HD), *parts, *refs, flops=4 * 1024 * 2560 * HD
    )
    got = swap(other, 1)

    send = call(send_kernel, (2, 4, 12, 16, HD), first, got)

    second, middle, refs, send = lax.optimization_barrier((second, middle, refs, send))
    second = second.reshape(16, 4, 6, 16, HD)
    by_frame = call(split_second_kernel, (16, 4, 6, 16, HD), second)
    other = call(other_kernel, (4, 2, 4, 6, 16, HD), second)

    by_frame = lax.all_to_all(by_frame, YX, split_axis=0, concat_axis=0, tiled=True)

    bias = [pltpu.VMEM((256, 1024), jnp.float32)]
    mine, other = call(
        temporal_own_kernel, [(2, 16, 2, 16, HD)] * 2, second, swap(other, 1), scratch=bias
    )
    recv, mine, other = lax.optimization_barrier((swap(send, 2), mine, other))
    keep, send = call(
        temporal_middle_kernel, [(2, 16, 16, HD)] * 2, first, got, recv, scratch=bias
    )
    by_frame, other, send = lax.optimization_barrier((by_frame, other, send))
    back = swap(send, 2)
    other = swap(other, 1)
    middle_other = swap(jnp.stack((keep[1], back[1])), 1)

    spatial = call(
        spatial_second_kernel,
        (16, 4, 3, 16, HD),
        by_frame,
        *refs,
        middle,
        flops=8 * 1024 * 2560 * HD,
        in_spec=HBM,
        out_spec=HBM,
        vmem=62,
        scratch=[
            pltpu.VMEM((16, 4, 6, 16, HD), jnp.bfloat16),
            pltpu.VMEM((4, 4, 12, 16, HD), jnp.bfloat16),
            pltpu.VMEM((4, 4, 12, 16, HD), jnp.bfloat16),
            pltpu.VMEM((3, 16, 4, 16, HD), jnp.bfloat16),
            pltpu.SemaphoreType.DMA((16,)),
        ],
    )
    spatial = lax.all_to_all(spatial, YX, split_axis=0, concat_axis=0, tiled=True)

    attended = call(
        sum_kernel, (16, 4, 3, 16, HD), spatial, mine, other, keep, back, middle_other
    )
    attended = lax.all_to_all(attended, Z, split_axis=0, concat_axis=0, tiled=True)
    return call(unpack_kernel, queries.shape, attended)


def solution(mesh):
    axes = ("zl1", "zl0", "core", "y", "zh1", "zh0", "x")
    split = Mesh(mesh.devices.reshape(2, 2, 2, 4, 2, 2, 4), axes)
    rows = P(axes[:3], axes[3:], None)
    refs = P(axes, None)
    return jax.shard_map(
        local,
        mesh=split,
        in_specs=(rows, rows, rows, refs, refs),
        out_specs=rows,
        check_vma=False,
    )
```

```python
import math

import jax
import jax.numpy as jnp
from jax import lax
from jax.experimental import pallas as pl
from jax.experimental.pallas import tpu as pltpu
from jax.sharding import Mesh, PartitionSpec as P

HD = 128
LOG2E = 1.4426950408889634
Z = ("zh1", "zl1", "zl0", "zh0")
YX = ("y", "x")
VMEM = pl.BlockSpec(memory_space=pltpu.VMEM)
HBM = pl.BlockSpec(memory_space=pltpu.HBM)


def z_index(zl, zh1, zh0):
    at = {"zl1": zl // 2, "zl0": zl % 2, "zh1": zh1, "zh0": zh0}
    return at[Z[0]] * 8 + at[Z[1]] * 4 + at[Z[2]] * 2 + at[Z[3]]


def chip_of(index):
    at = {axis: index >> (3 - i) & 1 for i, axis in enumerate(Z)}
    return at["zl1"], at["zl0"], at["zh1"] * 2 + at["zh0"]


def head_of(index, middle):
    zl1, zl0, zh = chip_of(index)
    return (zh * 2 + zl1) * 3 + (1 if middle else 2 * zl0)


def frame_of(index, j, slot):
    return 4 * chip_of(index)[1] + j if slot == 2 else 2 * j + slot


def columns(head):
    return slice(head * HD, (head + 1) * HD)


def pack_first_kernel(q_ref, k_ref, v_ref, ref_key_ref, ref_value_ref, out_hbm, out_ref, key_rows, value_rows, sems):
    rows = [
        pltpu.make_async_copy(ref_key_ref, key_rows, sems.at[64]),
        pltpu.make_async_copy(ref_value_ref, value_rows, sems.at[65]),
    ]
    reads, writes = [], []
    for z in range(16):
        for t, ref in enumerate((q_ref, k_ref, v_ref)):
            frames = pl.ds(frame_of(z, 0, 2), 4)
            source = ref.at[frames, :, pl.ds(head_of(z, True) * HD, HD)]
            target = out_ref.at[z, pl.ds(t * 4, 4)]
            reads.append(pltpu.make_async_copy(source, target, sems.at[z * 4 + t]))
        writes.append(pltpu.make_async_copy(out_ref.at[z], out_hbm.at[z], sems.at[z * 4 + 3]))
    for copy in rows + reads:
        copy.start()
    for copy in rows:
        copy.wait()
    for z in range(16):
        for t, ref in enumerate((key_rows, value_rows)):
            for middle in range(2):
                at = (t * 2 + middle) * 4
                out_ref[z, 12, at : at + 3] = ref[:, columns(head_of(z, middle))]
        for copy in reads[z * 3 : z * 3 + 3]:
            copy.wait()
        writes[z].start()
    for copy in writes:
        copy.wait()


def pack_second_kernel(q_ref, k_ref, v_ref, out_ref):
    for z in range(16):
        for j in range(4):
            for slot in range(2):
                for t, ref in enumerate((q_ref, k_ref, v_ref)):
                    out_ref[z, j, t, slot] = ref[frame_of(z, j, slot), :, columns(head_of(z, False))]


def split_first_kernel(in_ref, *outs):
    *part_refs, other_ref, rows_ref = outs
    y, x, core = lax.axis_index("y"), lax.axis_index("x"), lax.axis_index("core")
    for zl in range(4):
        for half in range(2):
            other_ref[zl, half] = in_ref[z_index(zl, 1 - core, half), :12]
    for z in range(16):
        for t in range(2):
            for middle in range(2):
                at = (t * 2 + middle) * 4
                rows_ref[t, middle, z * 3 : z * 3 + 3] = in_ref[z, 12, at : at + 3]
    rows = rows_ref[...].reshape(12, 16, HD)
    for k, part_ref in enumerate(part_refs):
        zl = lax.rem(y + k, 4)
        for m in range(4):
            j = lax.rem(x + m, 4)
            for zh in range(4):
                for t in range(3):
                    part_ref[m, zh * 3 + t] = in_ref[z_index(zl, zh // 2, zh % 2), t * 4 + j]
        part_ref[4] = rows


def send_kernel(first_ref, got_ref, out_ref):
    core, half = lax.axis_index("core"), 1 - lax.axis_index("zl0")
    for zl in range(4):
        out_ref[0, zl] = first_ref[z_index(zl, core, half), :12]
        out_ref[1, zl] = got_ref[zl, half]


def split_second_kernel(in_ref, frame_ref):
    for zl in range(4):
        for zh in range(4):
            for j in range(4):
                frame_ref[zl * 4 + j, zh] = in_ref[z_index(zl, zh // 2, zh % 2), j]


def other_kernel(in_ref, other_ref):
    core = lax.axis_index("core")
    for zl in range(4):
        for half in range(2):
            other_ref[zl, half] = in_ref[z_index(zl, 1 - core, half)]


def token_bias(bias_ref):
    rows = lax.broadcasted_iota(jnp.int32, bias_ref.shape, 0)
    columns = lax.broadcasted_iota(jnp.int32, bias_ref.shape, 1)
    bias_ref[...] = jnp.where(((rows ^ columns) & 15) == 0, 0.0, -1e30)


def attend_tokens(queries, keys, values, bias_ref):
    scale = LOG2E / math.sqrt(HD)
    key, value = jnp.concatenate(keys), jnp.concatenate(values)
    for query in queries:
        scores = lax.dot_general(
            query, key, (((1,), (1,)), ((), ())), preferred_element_type=jnp.float32
        )
        scores += bias_ref[...]
        highest = jnp.max(scores, axis=1, keepdims=True)
        weights = jnp.exp2((scores - highest) * scale)
        totals = jnp.sum(weights, axis=1, keepdims=True)
        result = jnp.dot(weights.astype(jnp.bfloat16), value, preferred_element_type=jnp.float32)
        yield (result / totals).astype(jnp.bfloat16).reshape(16, 16, HD)


def temporal_middle_kernel(first_ref, got_ref, recv_ref, keep_ref, send_ref, bias_ref):
    core, half = lax.axis_index("core"), lax.axis_index("zl0")
    token_bias(bias_ref)

    def block(part, t):
        at = slice(t * 4, t * 4 + 4)
        if part == 0:
            tiles = [first_ref[z_index(zl, core, half), at] for zl in range(4)]
        elif part == 1:
            tiles = [got_ref[zl, half, at] for zl in range(4)]
        else:
            tiles = [recv_ref[part - 2, zl, at] for zl in range(4)]
        return jnp.concatenate(tiles).reshape(256, HD)

    tensors = [[block(part, t) for part in range(4)] for t in range(3)]
    for part, result in enumerate(attend_tokens(*tensors, bias_ref)):
        (keep_ref if part < 2 else send_ref)[part % 2] = result


def temporal_own_kernel(in_ref, got_ref, mine_ref, other_ref, bias_ref):
    core = lax.axis_index("core")
    token_bias(bias_ref)
    for half in range(2):

        def block(part, slot, t):
            if part == 0:
                tiles = [in_ref[z_index(zl, core, half), :, t * 2 + slot] for zl in range(4)]
            else:
                tiles = [got_ref[zl, half, :, t * 2 + slot] for zl in range(4)]
            return jnp.concatenate(tiles).reshape(256, HD)

        blocks = [(part, slot) for part in range(2) for slot in range(2)]
        tensors = [[block(part, slot, t) for part, slot in blocks] for t in range(3)]
        for (part, slot), result in zip(blocks, attend_tokens(*tensors, bias_ref)):
            (other_ref if part else mine_ref)[slot, :, half] = result


def score(query, keys):
    nt = (((1,), (1,)), ((), ()))
    return [lax.dot_general(query, key, nt, preferred_element_type=jnp.float32) for key in keys]


def weigh(scores, values):
    scale = LOG2E / math.sqrt(HD)
    highest = [jnp.max(part, axis=1, keepdims=True) for part in scores]
    highest = jnp.maximum(*highest)
    weights = [jnp.exp2((part - highest) * scale).astype(jnp.bfloat16) for part in scores]
    result = [
        jnp.dot(part, value, preferred_element_type=jnp.float32)
        for part, value in zip(weights, values)
    ]
    result = result[0] + result[1]
    return (result[:, :HD] / result[:, HD:]).astype(jnp.bfloat16)


def with_ones(value):
    return jnp.concatenate((value, jnp.ones_like(value)), axis=1)


def ref_rows(mine_ref, other_ref, t, middle):
    at = t * 6 + middle * 3
    parts = [ref[:, :, at : at + 3].reshape(768, HD) for ref in (mine_ref, other_ref)]
    return jnp.concatenate(parts)


def spatial_first_kernel(*refs):
    *parts, mine_ref, other_ref, out_ref = refs
    y, x = lax.axis_index("y"), lax.axis_index("x")

    def tensor(part, t):
        return jnp.stack([part[0, :, zh * 3 + t] for zh in range(4)], axis=1).reshape(256, HD)

    own_k = jnp.concatenate([tensor(part, 1) for part in parts])
    own_v = with_ones(jnp.concatenate([tensor(part, 2) for part in parts]))
    keys = own_k, ref_rows(mine_ref, other_ref, 0, 1)
    values = own_v, with_ones(ref_rows(mine_ref, other_ref, 1, 1))
    for m, part in enumerate(parts):
        result = weigh(score(tensor(part, 0), keys), values)
        result = result.reshape(4, 4, 16, HD)
        for k in range(4):
            out_ref[lax.rem(y + 4 - k, 4) * 4 + lax.rem(x + 4 - m, 4)] = result[k]


def spatial_second_kernel(x_hbm, mine_hbm, other_hbm, first_hbm, out_hbm, x_ref, mine_ref, other_ref, out_ref, sems):
    moves = [(first_hbm, out_ref.at[2])]
    for start, blocks, source, target in (
        (0, 4, x_hbm, x_ref),
        (0, 3, mine_hbm, mine_ref),
        (0, 3, other_hbm, other_ref),
        (4, 2, x_hbm, x_ref),
        (6, 3, mine_hbm, mine_ref),
        (6, 3, other_hbm, other_ref),
    ):
        at = pl.ds(start, blocks)
        moves.append((source.at[:, :, at], target.at[:, :, at]))
    passed, *copies = [pltpu.make_async_copy(*move, sems.at[i]) for i, move in enumerate(moves)]
    for copy in copies:
        copy.start()
    passed.start()
    for copy in copies[:3]:
        copy.wait()
    ref_k = ref_rows(mine_ref, other_ref, 0, 0)
    blocks = [(slot, slice(at, at + 4)) for slot in range(2) for at in range(0, 16, 4)]

    def scores(slot, at):
        keys = x_ref[:, :, 2 + slot].reshape(1024, HD), ref_k
        return score(x_ref[at, :, slot].reshape(256, HD), keys)

    later = scores(*blocks[0])
    for copy in copies[3:]:
        copy.wait()
    ref_v = with_ones(ref_rows(mine_ref, other_ref, 1, 0))
    passed.wait()
    writes = [pltpu.make_async_copy(out_ref.at[2], out_hbm.at[:, :, 2], sems.at[15])]
    writes[0].start()
    for i, (slot, at) in enumerate(blocks):
        now, later = later, scores(*blocks[i + 1]) if i < 7 else None
        result = weigh(now, (with_ones(x_ref[:, :, 4 + slot].reshape(1024, HD)), ref_v))
        out_ref[slot, at] = result.reshape(4, 4, 16, HD)
        target = out_hbm.at[pl.ds(at.start, 4), :, slot]
        writes.append(pltpu.make_async_copy(out_ref.at[slot, pl.ds(at.start, 4)], target, sems.at[7 + i]))
        writes[-1].start()
    for write in writes:
        write.wait()


def sum_kernel(spatial_ref, mine_ref, other_ref, keep_ref, back_ref, middle_ref, out_ref):
    core, zl0 = lax.axis_index("core"), lax.axis_index("zl0")

    def add(group, zh1, zh0, slot, temporal):
        both = spatial_ref[group, zh1 * 2 + zh0, slot].astype(jnp.float32) + temporal.astype(jnp.float32)
        out_ref[z_index(group // 4, zh1, zh0), group % 4, slot] = both.astype(jnp.bfloat16)

    for group in range(16):
        for half in range(2):
            for slot in range(2):
                add(group, core, half, slot, mine_ref[slot, group, half])
                add(group, 1 - core, half, slot, other_ref[slot, group, half])
        add(group, core, zl0, 2, keep_ref[0, group])
        add(group, core, 1 - zl0, 2, back_ref[0, group])
        add(group, 1 - core, zl0, 2, middle_ref[0, group])
        add(group, 1 - core, 1 - zl0, 2, middle_ref[1, group])


def unpack_kernel(in_ref, out_ref):
    for z in range(16):
        for j in range(4):
            for slot in range(3):
                out_ref[frame_of(z, j, slot), :, columns(head_of(z, slot == 2))] = in_ref[z, j, slot]


def call(kernel, out_shapes, *args, flops=0, scratch=(), in_spec=VMEM, out_spec=VMEM, vmem=32):
    several = isinstance(out_shapes, list)
    shapes = [jax.ShapeDtypeStruct(s, jnp.bfloat16) for s in (out_shapes if several else [out_shapes])]
    size = sum(a.size * 2 for a in args) + sum(2 * math.prod(s.shape) for s in shapes)
    cost = pl.CostEstimate(flops=flops, bytes_accessed=size, transcendentals=0)
    return pl.pallas_call(
        kernel,
        out_shape=shapes if several else shapes[0],
        in_specs=[in_spec] * len(args),
        out_specs=[VMEM] * len(shapes) if several else out_spec,
        scratch_shapes=scratch,
        compiler_params=pltpu.CompilerParams(vmem_limit_bytes=vmem * 1024 * 1024),
        cost_estimate=cost,
    )(*args)


def swap(tensor, mask):
    return lax.ppermute(tensor, ("zl0", "core"), [(i, i ^ mask) for i in range(4)])


def shift(tensor, axis, step):
    return lax.ppermute(tensor, axis, [(i, (i + step) % 4) for i in range(4)])


def local(queries, keys, values, ref_keys, ref_values):
    first = call(
        pack_first_kernel,
        (16, 13, 16, HD),
        queries,
        keys,
        values,
        ref_keys,
        ref_values,
        in_spec=HBM,
        out_spec=HBM,
        vmem=62,
        scratch=[
            pltpu.VMEM((16, 13, 16, HD), jnp.bfloat16),
            pltpu.VMEM(ref_keys.shape, jnp.bfloat16),
            pltpu.VMEM(ref_keys.shape, jnp.bfloat16),
            pltpu.SemaphoreType.DMA((66,)),
        ],
    )
    first = lax.all_to_all(first, Z, split_axis=0, concat_axis=0, tiled=True)
    second = call(pack_second_kernel, (16, 4, 3, 2, 16, HD), queries, keys, values)
    first, second = lax.optimization_barrier((first, second))
    second = lax.all_to_all(second, Z, split_axis=0, concat_axis=0, tiled=True)

    *parts, other = call(
        split_first_kernel,
        [(5, 12, 16, HD)] * 4 + [(4, 2, 12, 16, HD)],
        first,
        scratch=[pltpu.VMEM((2, 2, 48, HD), jnp.bfloat16)],
    )
    parts = [parts[0]] + [shift(parts[step], "y", step) for step in (1, 2, 3)]
    rows = [part[4] for part in parts]
    parts = [jnp.stack([part[m] for part in parts] + rows).reshape(2, 4, 12, 16, HD) for m in range(4)]
    parts = [parts[0]] + [shift(parts[step], "x", step) for step in (1, 2, 3)]
    my_refs = jnp.stack([part[1] for part in parts])
    refs = (my_refs, lax.ppermute(my_refs, "core", [(0, 1), (1, 0)]))
    middle = call(
        spatial_first_kernel, (16, 4, 16, HD), *parts, *refs, flops=4 * 1024 * 2560 * HD
    )
    got = swap(other, 1)

    send = call(send_kernel, (2, 4, 12, 16, HD), first, got)

    second, middle, refs, send = lax.optimization_barrier((second, middle, refs, send))
    second = second.reshape(16, 4, 6, 16, HD)
    by_frame = call(split_second_kernel, (16, 4, 6, 16, HD), second)
    other = call(other_kernel, (4, 2, 4, 6, 16, HD), second)

    by_frame = lax.all_to_all(by_frame, YX, split_axis=0, concat_axis=0, tiled=True)

    bias = [pltpu.VMEM((256, 1024), jnp.float32)]
    mine, other = call(
        temporal_own_kernel, [(2, 16, 2, 16, HD)] * 2, second, swap(other, 1), scratch=bias
    )
    recv, mine, other = lax.optimization_barrier((swap(send, 2), mine, swap(other, 1)))
    keep, send = call(
        temporal_middle_kernel, [(2, 16, 16, HD)] * 2, first, got, recv, scratch=bias
    )
    by_frame, send = lax.optimization_barrier((by_frame, send))
    back = swap(send, 2)
    middle_other = swap(jnp.stack((keep[1], back[1])), 1)

    spatial = call(
        spatial_second_kernel,
        (16, 4, 3, 16, HD),
        by_frame,
        *refs,
        middle,
        flops=8 * 1024 * 2560 * HD,
        in_spec=HBM,
        out_spec=HBM,
        vmem=62,
        scratch=[
            pltpu.VMEM((16, 4, 6, 16, HD), jnp.bfloat16),
            pltpu.VMEM((4, 4, 12, 16, HD), jnp.bfloat16),
            pltpu.VMEM((4, 4, 12, 16, HD), jnp.bfloat16),
            pltpu.VMEM((3, 16, 4, 16, HD), jnp.bfloat16),
            pltpu.SemaphoreType.DMA((16,)),
        ],
    )
    spatial = lax.all_to_all(spatial, YX, split_axis=0, concat_axis=0, tiled=True)

    attended = call(
        sum_kernel, (16, 4, 3, 16, HD), spatial, mine, other, keep, back, middle_other
    )
    attended = lax.all_to_all(attended, Z, split_axis=0, concat_axis=0, tiled=True)
    return call(unpack_kernel, queries.shape, attended)


def solution(mesh):
    axes = ("zl1", "zl0", "core", "y", "zh1", "zh0", "x")
    split = Mesh(mesh.devices.reshape(2, 2, 2, 4, 2, 2, 4), axes)
    rows = P(axes[:3], axes[3:], None)
    refs = P(axes, None)
    return jax.shard_map(
        local,
        mesh=split,
        in_specs=(rows, rows, rows, refs, refs),
        out_specs=rows,
        check_vma=False,
    )
```
